32 devices in a mesh: chain: 4 (over y, x), tok: 8 (over z, core).
Axes of the slice: x: 2, y: 2, z: 4, core: 2. Of those that a mesh axis runs over, the one named last changes fastest.
Arguments:
- layer_activations: bfloat16 [2048, 8192], P('tok'), may hold values from -6 to 6
- rotated_probes: bfloat16 [2048, 8192], P('tok'), may hold values from -6 to 6
- attended_contents: bfloat16 [2048, 1024], P('tok'), may hold values from -6 to 6
- attended_slope: bfloat16 [2048, 8192], P('tok'), may hold values from -6 to 6
- locked_projection: bfloat16 [8192, 1024], P('tok', 'chain'), may hold values from -0.044194174 to 0.044194174
- first_multipliers: float32 [8, 8192, 64], P('chain', 'tok'), may hold values from -6 to 6
- second_multipliers: float32 [8, 64, 1024], P('chain', None, 'tok'), may hold values from -6 to 6
- first_jitter: float32 [8, 8192, 64], P('chain', 'tok'), may hold values from -6 to 6
- second_jitter: float32 [8, 64, 1024], P('chain', None, 'tok'), may hold values from -6 to 6
- chain_heats: float32 [8], P('chain'), may hold values from 0.05 to 1
- donor_chain: int32 [8], replicated, may hold values from 0 to 7, each once
Outputs:
- new_a: float32 [8, 8192, 64], P('chain', 'tok')
- new_b: float32 [8, 64, 1024], P('chain', None, 'tok')
The draws below stay inside these ranges and needn't reach their ends.
All inputs are finite; a program needn't handle non-finite values.
Results may differ from the reference program's by a relative error of at most 0.019.
Values may be sent and summed in bfloat16 or wider, within the bound.
No kernel may reach another device: no remote copies, remote signals or barrier semaphores. Data moves between devices by JAX's collectives and lax.ppermute only.
A program may use at most 128 MiB of HBM per device.

```python
import math
import jax
import jax.numpy as jnp
from jax import lax

MODEL_WIDTH = 8192
QUERY_HEADS = 64
KEY_HEADS = 8
HEAD_SIZE = 128
ADAPTER_RANK = 64
SEQUENCE_TOKENS = 256
KEY_WIDTH = 1024
CHAIN_NUMBER = 8
TOKEN_TOTAL = 2048


def draw_weight_matrix(key):
    weight_key = jax.random.fold_in(key, 101)
    return jax.random.truncated_normal(weight_key, -4.0, 4.0, (MODEL_WIDTH, KEY_WIDTH), jnp.float32) * (1.0 / math.sqrt(MODEL_WIDTH))


def hot_layout(key):
    sequence_count = TOKEN_TOTAL // SEQUENCE_TOKENS
    query_group = QUERY_HEADS // KEY_HEADS
    weight = draw_weight_matrix(key)
    weight_low = weight.astype(jnp.bfloat16).astype(jnp.float32)
    seq_ids = jnp.arange(sequence_count, dtype=jnp.int32)
    is_hot = seq_ids % 3 == 0
    level = 3.0 + 1.5 * (seq_ids // 3 % 3).astype(jnp.float32)
    row_noise = jax.random.normal(jax.random.fold_in(key, 102), (sequence_count, MODEL_WIDTH), jnp.float32)
    first_row = (level[:, None] * jnp.tanh(2.0 * row_noise)).astype(jnp.bfloat16).astype(jnp.float32)
    drawn_rows = jnp.dot(first_row, weight_low, precision=lax.Precision.HIGHEST)
    per_head_keys = drawn_rows.reshape(sequence_count, KEY_HEADS, 1, HEAD_SIZE)
    head_factor = jax.random.uniform(jax.random.fold_in(key, 103), (sequence_count, KEY_HEADS, query_group, 1), jnp.float32, 0.6, 1.0)
    hot_query = 6.0 * head_factor * jnp.tanh(2.0 * per_head_keys / level[:, None, None, None])
    score_top = jnp.max(jnp.sum(hot_query * per_head_keys, axis=-1), axis=(1, 2)) / math.sqrt(HEAD_SIZE)
    shrink = 1.0 - 2.0 / jnp.maximum(score_top, 4.0)
    second_row = shrink[:, None] * first_row
    return (is_hot, first_row, second_row, hot_query.reshape(sequence_count, QUERY_HEADS * HEAD_SIZE))


def draw_locked_projection(key, part):
    return draw_weight_matrix(key).astype(jnp.bfloat16)


def draw_layer_activations(key, part):
    sequence_count = TOKEN_TOTAL // SEQUENCE_TOKENS
    is_hot, first_row, second_row, hot_query = hot_layout(key)
    drawn = jax.random.truncated_normal(jax.random.fold_in(key, 104), -6.0, 6.0, (sequence_count, SEQUENCE_TOKENS, MODEL_WIDTH), jnp.float32)
    position = jnp.arange(SEQUENCE_TOKENS, dtype=jnp.int32)[None, :, None]
    hot = is_hot[:, None, None]
    drawn = jnp.where(hot & (position == SEQUENCE_TOKENS - 4), first_row[:, None, :], drawn)
    drawn = jnp.where(hot & (position == SEQUENCE_TOKENS - 3), second_row[:, None, :], drawn)
    return drawn.reshape(TOKEN_TOTAL, MODEL_WIDTH).astype(jnp.bfloat16)


def draw_rotated_probes(key, part):
    sequence_count = TOKEN_TOTAL // SEQUENCE_TOKENS
    is_hot, first_row, second_row, hot_query = hot_layout(key)
    drawn = jax.random.truncated_normal(jax.random.fold_in(key, 105), -6.0, 6.0, (sequence_count, SEQUENCE_TOKENS, QUERY_HEADS * HEAD_SIZE), jnp.float32)
    position = jnp.arange(SEQUENCE_TOKENS, dtype=jnp.int32)[None, :, None]
    hot = is_hot[:, None, None]
    drawn = jnp.where(hot & (position == SEQUENCE_TOKENS - 2), hot_query[:, None, :], drawn)
    drawn = jnp.where(hot & (position == SEQUENCE_TOKENS - 1), 0.8 * hot_query[:, None, :], drawn)
    return drawn.reshape(TOKEN_TOTAL, QUERY_HEADS * HEAD_SIZE).astype(jnp.bfloat16)


def level_of(rng, dims, cuts, smallest, largest):
    factor_of, own = 1.0, jax.random.fold_in(rng, 6)
    for dim, blocks in cuts:
        draws = jnp.exp(jax.random.uniform(jax.random.fold_in(own, dim), (blocks,), jnp.float32, smallest / len(cuts), largest / len(cuts)))
        factor_of = factor_of * jnp.repeat(draws, dims[dim] // blocks).reshape([-1 if axis == dim else 1 for axis in range(len(dims))])
    return factor_of


def gaussian(rng, extent, width, reach, split=(), kind=jnp.bfloat16):
    drawn = jax.random.normal(rng, extent, jnp.float32) * width
    if len(split) > 0:
        drawn = level_of(rng, extent, split, -0.22, 0.18) * drawn
    return jnp.clip(drawn, min=-reach, max=reach).astype(kind)


def setup_inputs(seed: int = 0) -> dict:
    arg_keys = jax.random.split(jax.random.key(seed), 12)
    return {
        "layer_activations": draw_layer_activations(jax.random.fold_in(arg_keys[11], 71), 0),
        "rotated_probes": draw_rotated_probes(jax.random.fold_in(arg_keys[11], 71), 0),
        "attended_contents": gaussian(arg_keys[2], (TOKEN_TOTAL, KEY_WIDTH), 1.0, 6.0, ((0, 8),)),
        "attended_slope": gaussian(arg_keys[3], (TOKEN_TOTAL, QUERY_HEADS * HEAD_SIZE), 1.0, 6.0, ((0, 8),)),
        "locked_projection": draw_locked_projection(jax.random.fold_in(arg_keys[11], 71), 0),
        "first_multipliers": gaussian(arg_keys[5], (CHAIN_NUMBER, MODEL_WIDTH, ADAPTER_RANK), 1.0, 6.0, ((0, 4), (1, 8)), jnp.float32),
        "second_multipliers": gaussian(arg_keys[6], (CHAIN_NUMBER, ADAPTER_RANK, KEY_WIDTH), 1.0, 6.0, ((0, 4), (2, 8)), jnp.float32),
        "first_jitter": gaussian(arg_keys[7], (CHAIN_NUMBER, MODEL_WIDTH, ADAPTER_RANK), 1.0, 6.0, ((0, 4), (1, 8)), jnp.float32),
        "second_jitter": gaussian(arg_keys[8], (CHAIN_NUMBER, ADAPTER_RANK, KEY_WIDTH), 1.0, 6.0, ((0, 4), (2, 8)), jnp.float32),
        "chain_heats": jnp.clip(jnp.exp(math.log(1.0) - 2.9957323 * jax.random.uniform(arg_keys[9], (CHAIN_NUMBER,), jnp.float32) ** level_of(arg_keys[9], (CHAIN_NUMBER,), ((0, 4),), -0.2, 0.2)), 0.05, 1.0),
        "donor_chain": jax.random.permutation(arg_keys[10], CHAIN_NUMBER).astype(jnp.int32),
    }


STRIDE_LENGTH = 0.2

def key_gradient(query_item, key_item, value_item, grad_item):
    score_scale = 1.0 / math.sqrt(HEAD_SIZE)
    query_f = query_item.astype(jnp.float32)
    scores = jnp.einsum('tjd,sd->jts', query_f, key_item.astype(jnp.float32)) * score_scale
    length = key_item.shape[0]
    future_mask = lax.broadcasted_iota(jnp.int32, (length, length), 1) > lax.broadcasted_iota(jnp.int32, (length, length), 0)
    scores = jnp.where(future_mask[None], -1e+30, scores)
    row_max = lax.optimization_barrier(jnp.max(scores, axis=-1, keepdims=True))
    expo = jnp.exp(scores - row_max)
    attn_weights = expo / lax.optimization_barrier(jnp.sum(expo, axis=-1, keepdims=True))
    dweights = jnp.einsum('tjd,sd->jts', grad_item.astype(jnp.float32), value_item.astype(jnp.float32))
    center = lax.optimization_barrier(jnp.sum(attn_weights * dweights, axis=-1, keepdims=True))
    dscores = (attn_weights * (dweights - center)).astype(jnp.bfloat16)
    return jnp.einsum('jts,tjd->sd', dscores.astype(jnp.float32), query_f) * score_scale

def head_items(numeric_array, sequence_count, query_group):
    return numeric_array.reshape(sequence_count, SEQUENCE_TOKENS, KEY_HEADS, query_group, HEAD_SIZE).transpose(0, 2, 1, 3, 4).reshape(sequence_count * KEY_HEADS, SEQUENCE_TOKENS, query_group, HEAD_SIZE)

def key_items(numeric_array, sequence_count):
    return numeric_array.reshape(sequence_count, SEQUENCE_TOKENS, KEY_HEADS, HEAD_SIZE).transpose(0, 2, 1, 3).reshape(sequence_count * KEY_HEADS, SEQUENCE_TOKENS, HEAD_SIZE)

def reference(layer_activations, rotated_probes, attended_contents, attended_slope, locked_projection, first_multipliers, second_multipliers, first_jitter, second_jitter, chain_heats, donor_chain):
    adapter_scale = 1.0 / math.sqrt(MODEL_WIDTH * ADAPTER_RANK)
    sequence_count = TOKEN_TOTAL // SEQUENCE_TOKENS
    query_group = QUERY_HEADS // KEY_HEADS
    query_tensor = head_items(rotated_probes, sequence_count, query_group)
    gradient_total = head_items(attended_slope, sequence_count, query_group)
    value_tensor = key_items(attended_contents, sequence_count)
    plain_keys = jnp.dot(layer_activations, locked_projection, preferred_element_type=jnp.float32).astype(jnp.bfloat16)
    contract_product = (((0,), (0,)), ((), ()))

    def one_chain(chain_ordinal):
        a_low = first_multipliers[chain_ordinal].astype(jnp.bfloat16)
        right_low_rank = second_multipliers[chain_ordinal].astype(jnp.bfloat16)
        low_rank_keys = jnp.dot(layer_activations, a_low, preferred_element_type=jnp.float32).astype(jnp.bfloat16)
        key_rows = (plain_keys.astype(jnp.float32) + adapter_scale * jnp.dot(low_rank_keys, right_low_rank, preferred_element_type=jnp.float32)).astype(jnp.bfloat16)
        key_tensor = key_items(key_rows, sequence_count)
        step_result = lax.map(lambda items: key_gradient(*items), (query_tensor, key_tensor, value_tensor, gradient_total))
        key_input_gradient = step_result.reshape(sequence_count, KEY_HEADS, SEQUENCE_TOKENS, HEAD_SIZE).transpose(0, 2, 1, 3).reshape(TOKEN_TOTAL, KEY_WIDTH).astype(jnp.bfloat16)
        low_rank_gradient = (adapter_scale * jnp.dot(key_input_gradient, right_low_rank.T, preferred_element_type=jnp.float32)).astype(jnp.bfloat16)
        first_slope = lax.dot_general(layer_activations, low_rank_gradient, contract_product, preferred_element_type=jnp.float32)
        second_slope = adapter_scale * lax.dot_general(low_rank_keys, key_input_gradient, contract_product, preferred_element_type=jnp.float32)
        chain_heat = jnp.sqrt(2.0 * STRIDE_LENGTH * chain_heats[chain_ordinal])
        shifted_first = first_multipliers[chain_ordinal] - STRIDE_LENGTH * (first_slope + first_multipliers[chain_ordinal]) + chain_heat * first_jitter[chain_ordinal]
        shifted_second = second_multipliers[chain_ordinal] - STRIDE_LENGTH * (second_slope + second_multipliers[chain_ordinal]) + chain_heat * second_jitter[chain_ordinal]
        return (shifted_first, shifted_second)
    shifted_first, shifted_second = lax.map(one_chain, jnp.arange(CHAIN_NUMBER, dtype=jnp.int32))
    return (shifted_first[donor_chain], shifted_second[donor_chain])
```

```python
import math, functools
import jax, jax.numpy as jnp
from jax import lax
from jax.experimental import pallas as pl
from jax.experimental.pallas import tpu as pltpu
HD=128; RANK=64
LOG2E=1.4426950408889634
f32=jnp.float32; bf16=jnp.bfloat16
NT=(((1,),(1,)),((),()))
NN=(((1,),(0,)),((),()))
TN=(((0,),(0,)),((),()))

def dot(a,b,dims):
    return lax.dot_general(a,b,dims,preferred_element_type=f32)

def attention_kernel(scale, nchain, group, pair, pos_ref, q_ref, do_ref, v_ref, base_ref, lr_ref, b_ref, lg_ref, rt_ref, acc_ref):
    T = q_ref.shape[0]
    nb = T // 128
    ss = 1.0 / math.sqrt(HD)
    step = pl.program_id(0)

    @pl.when(step == 0)
    def _():
        acc_ref[...] = jnp.zeros_like(acc_ref)

    per_head = HD // b_ref.shape[2]
    b = jnp.concatenate([b_ref[pos_ref[1 + step * per_head + i]] for i in range(per_head)], axis=1)
    b = [b[c * RANK:(c + 1) * RANK] for c in range(nchain)]
    lr = [lr_ref[:, c * RANK:(c + 1) * RANK] for c in range(nchain)]
    keys = [(base_ref[0].astype(f32) + scale * dot(lr[c], b[c], NN)).astype(bf16) for c in range(nchain)]
    keys = [jnp.concatenate([x[j * 128:(j + 1) * 128] for x in keys], axis=0) for j in range(nb)]
    row = lax.broadcasted_iota(jnp.int32, (128, 128), 0)
    col = lax.broadcasted_iota(jnp.int32, (128, 128), 1)
    future = row > col
    v = v_ref[...]
    kg = [jnp.zeros((nchain * 128, HD), f32) for _ in range(nb)]
    for h0 in range(0, group, pair):
        def heads(ref, j):
            return jnp.concatenate([ref[j * 128:, (h0 + h) * HD:(h0 + h + 1) * HD] for h in range(pair)], axis=0)

        qs = [heads(q_ref, j) for j in range(nb)]
        dp = [dot(v[j * 128:(j + 1) * 128], heads(do_ref, j), NT) for j in range(nb)]
        s = [dot(keys[j], qs[j], NT) for j in range(nb)]
        ds = [[[None] * (pair * (nb - j)) for _ in range(nchain)] for j in range(nb)]
        for h in range(pair):
            for c in range(nchain):
                for i in range(nb):
                    def at(x, j, c):
                        k = h * (nb - j) + i - j
                        return x[j][c * 128:(c + 1) * 128, k * 128:(k + 1) * 128]

                    blocks = [at(s, j, c) for j in range(i + 1)]
                    blocks[i] = jnp.where(future, -1e30, blocks[i])
                    top = jnp.max(functools.reduce(jnp.maximum, blocks), axis=0, keepdims=True)
                    e = [jnp.exp2((x - top) * (ss * LOG2E)) for x in blocks]
                    d = [at(dp, j, 0) for j in range(i + 1)]
                    r = 1.0 / jnp.sum(functools.reduce(jnp.add, e), axis=0, keepdims=True)
                    center = r * jnp.sum(functools.reduce(jnp.add, [x * y for x, y in zip(e, d)]), axis=0, keepdims=True)
                    for j in range(i + 1):
                        ds[j][c][h * (nb - j) + i - j] = ((e[j] * r) * (d[j] - center)).astype(bf16)
        for j in range(nb):
            dsj = jnp.concatenate([jnp.concatenate(x, axis=1) for x in ds[j]], axis=0)
            kg[j] = kg[j] + dot(dsj, qs[j], NN)
    for c in range(nchain):
        g = (jnp.concatenate([x[c * 128:(c + 1) * 128] for x in kg], axis=0) * ss).astype(bf16)
        acc_ref[:, c * RANK:(c + 1) * RANK] += dot(g, b[c], NT)
        rt_ref[0, c] = scale * dot(lr[c], g, TN)

    @pl.when(step == pl.num_programs(0) - 1)
    def _():
        lg_ref[...] = (scale * acc_ref[...]).astype(lg_ref.dtype)


def attention(pos, q, do, v, base, lr, b, scale):
    T, KW = v.shape
    nchain = lr.shape[1] // RANK
    KH, group = KW // HD, q.shape[1] // KW
    hp = base.shape[2] // HD
    grid = pltpu.PrefetchScalarGridSpec(
        num_scalar_prefetch=1, grid=(KH,),
        in_specs=[
            pl.BlockSpec((T, group * HD), lambda g, p: (0, g)),
            pl.BlockSpec((T, group * HD), lambda g, p: (0, g)),
            pl.BlockSpec((T, HD), lambda g, p: (0, g)),
            pl.BlockSpec((1, T, HD), lambda g, p: (p[0] ^ (g // hp), 0, g % hp)),
            pl.BlockSpec(lr.shape, lambda g, p: (0, 0)),
            pl.BlockSpec(b.shape, lambda g, p: (0, 0, 0)),
        ],
        out_specs=[
            pl.BlockSpec(lr.shape, lambda g, p: (0, 0)),
            pl.BlockSpec((1, nchain, RANK, HD), lambda g, p: (g, 0, 0, 0)),
        ],
        scratch_shapes=[pltpu.VMEM(lr.shape, f32)],
    )
    return pl.pallas_call(
        functools.partial(attention_kernel, scale, nchain, group, 4), grid_spec=grid,
        out_shape=[jax.ShapeDtypeStruct(lr.shape, bf16), jax.ShapeDtypeStruct((KH, nchain, RANK, HD), f32)],
        compiler_params=pltpu.CompilerParams(vmem_limit_bytes=28 * 1024 * 1024),
        cost_estimate=pl.CostEstimate(flops=10_000_000_000, bytes_accessed=20_000_000, transcendentals=T * T * 64 * nchain),
        name="attention",
    )(pos, q, do, v, base, lr, b)


from jax.sharding import PartitionSpec as P

STRIDE_LENGTH = 0.2


def gradient_kernel(own, nrank, pos_ref, x_ref, lg_ref, rt_ref, out_ref):
    g = dot(lg_ref[...], x_ref[...], TN)
    for c in range(nrank // RANK):
        out_ref[0, c] = jnp.concatenate([g[c * RANK:(c + 1) * RANK], rt_ref[0, c]], axis=1).astype(out_ref.dtype)


def gradients(pos, x, lg, rt, n, dtype):
    T, width = x.shape
    nrank = lg.shape[1]
    shards = 2 * n
    heads, nchain, _, kcols = rt.shape
    cols, kcols = width // shards, heads * kcols // shards
    if heads != shards:
        rt = rt.reshape(heads, nchain, RANK, -1, kcols).transpose(0, 3, 1, 2, 4).reshape(shards, nchain, RANK, kcols)
    grid = pltpu.PrefetchScalarGridSpec(
        num_scalar_prefetch=1, grid=(n,),
        in_specs=[
            pl.BlockSpec((T, cols), lambda i, p: (0, p[i])),
            pl.BlockSpec((T, nrank), lambda i, p: (0, 0)),
            pl.BlockSpec((1, nchain, RANK, kcols), lambda i, p: (p[i], 0, 0, 0)),
        ],
        out_specs=pl.BlockSpec((1, nchain, RANK, cols + kcols), lambda i, p: (i, 0, 0, 0)),
    )
    return pl.pallas_call(
        functools.partial(gradient_kernel, n, nrank), grid_spec=grid,
        out_shape=jax.ShapeDtypeStruct((n, nchain, RANK, cols + kcols), dtype),
        compiler_params=pltpu.CompilerParams(vmem_limit_bytes=24 * 1024 * 1024),
        cost_estimate=pl.CostEstimate(flops=T * width * nrank, bytes_accessed=3_000_000, transcendentals=0),
        name="gradients",
    )(pos, x, lg, rt)


def reorder_kernel(pos_ref, x_ref, out_ref):
    out_ref[...] = x_ref[...]


def reorder(pos, x, cols):
    T, width = x.shape
    grid = pltpu.PrefetchScalarGridSpec(
        num_scalar_prefetch=1, grid=(width // cols,),
        in_specs=[pl.BlockSpec((T, cols), lambda i, p: (0, p[i]))],
        out_specs=pl.BlockSpec((T, cols), lambda i, p: (0, i)),
    )
    return pl.pallas_call(
        reorder_kernel, grid_spec=grid, out_shape=jax.ShapeDtypeStruct(x.shape, x.dtype),
        compiler_params=pltpu.CompilerParams(vmem_limit_bytes=8 * 1024 * 1024),
        cost_estimate=pl.CostEstimate(flops=0, bytes_accessed=4 * T * width, transcendentals=0), name="reorder",
    )(pos, x)


def per_device(layer_activations, rotated_probes, attended_contents, attended_slope, locked_projection,
               first_multipliers, second_multipliers, first_jitter, second_jitter, chain_heats, donor_chain):
    T, width = layer_activations.shape
    scale = 1.0 / math.sqrt(width * RANK)
    nchain, arows, _ = first_multipliers.shape
    nc = lax.axis_size("chain")
    nt = lax.axis_size("tok")
    nz = nt // 2
    p = lax.axis_index("chain")
    t = lax.axis_index("tok")
    z, core = t // 2, t % 2

    def shift(x, k):
        return lax.ppermute(x, "tok", [(i, (i + 2 * k) % nt) for i in range(nt)])

    def swap_cores(x):
        return lax.ppermute(x, "tok", [(i, i ^ 1) for i in range(nt)])

    def exchange(x, k):
        return lax.ppermute(x, "chain", [(i, i ^ k) for i in range(nc)])

    source = lax.dynamic_slice_in_dim(donor_chain, p * nchain, nchain)

    def take_slots(own):
        every = jnp.concatenate([own] + [exchange(own, k) for k in range(1, nc)])
        return jnp.concatenate([
            lax.dynamic_slice_in_dim(every, (source[j] // nchain ^ p) * nchain + source[j] % nchain, 1)
            for j in range(nchain)
        ])

    heat = jnp.sqrt(2.0 * STRIDE_LENGTH * chain_heats)[:, None, None]
    first = first_multipliers.transpose(0, 2, 1)
    pre_a = (1.0 - STRIDE_LENGTH) * first + heat * first_jitter.transpose(0, 2, 1)
    pre_b = (1.0 - STRIDE_LENGTH) * second_multipliers + heat * second_jitter
    kcols = second_multipliers.shape[2]

    half = arows // 2
    order = []
    for s in range(nz):
        for c in (core, 1 - core):
            order += [((z - s) % nz * 2 + c) * 2, ((z + s) % nz * 2 + c) * 2 + 1]
    x_ordered = reorder(jnp.stack(order).astype(jnp.int32), layer_activations, half)

    def both_cores(pieces, axis):
        here = jnp.concatenate(pieces, axis=axis)
        return jnp.concatenate([here, swap_cores(here)], axis=axis)

    def x_piece(s):
        return x_ordered[:, s * 2 * arows:(s + 1) * 2 * arows]

    w = (locked_projection[:half], locked_projection[half:])
    a = None
    plain = low_rank = 0.0
    b_low = []
    for s in range(nz + 1):
        if s < nz:
            plain = plain + jnp.dot(x_piece(s), both_cores(w, 0), preferred_element_type=f32)
        if a is not None:
            here = jnp.concatenate([a[0], a[1]], axis=1)
            there = swap_cores(here)
            parts = [here[:, :half], here[:, half + kcols:], there[:, :half], there[:, half + kcols:]]
            low_rank = low_rank + dot(x_piece(s - 1), jnp.concatenate(parts, axis=1), NT)
            b_low += [here[:, half:half + kcols], there[:, half:half + kcols]]
        if s < nz - 1:
            w = (shift(w[0], 1), shift(w[1], -1))
        if s == 0:
            ab = take_slots(jnp.concatenate([first[:, :, :half], second_multipliers, first[:, :, half:]], axis=2).astype(bf16))
            w, ab = lax.optimization_barrier((w, ab))
            ab = ab.reshape(nchain * RANK, arows + kcols)
            a = (ab[:, :half + kcols], ab[:, half + kcols:])
        elif s < nz:
            a = (shift(a[0], 1), shift(a[1], -1))
    plain = plain.astype(bf16)
    low_rank = low_rank.astype(bf16)
    base = jnp.stack([plain] + [exchange(plain, k) for k in range(1, nc)])
    shards = jnp.arange(nt, dtype=jnp.int32)
    places = (z - shards // 2) % nz * 2 + (shards % 2 != core).astype(jnp.int32)
    pos = jnp.concatenate([p[None], places]).astype(jnp.int32)
    rest = take_slots(jnp.concatenate([pre_a, pre_b], axis=2).astype(bf16))
    base, rest = lax.optimization_barrier((base, rest))

    low_grad, right = attention(pos, rotated_probes, attended_slope, attended_contents, base, low_rank, jnp.stack(b_low), scale)

    around = (z + jnp.arange(nz, dtype=jnp.int32)) % nz
    theirs = swap_cores(gradients(around * 2 + 1 - core, layer_activations, low_grad, right, nz, bf16))
    mine = gradients(around * 2 + core, layer_activations, low_grad, right, nz, f32)
    total = mine[0] + theirs[0]
    send = (mine[1:] + theirs[1:]).astype(bf16)
    for k in range(1, nz):
        total = total + shift(send[k - 1], k).astype(f32)
    new = rest.astype(f32) - STRIDE_LENGTH * total
    return new[:, :, :arows].transpose(0, 2, 1), new[:, :, arows:]


def solution(mesh):
    return jax.shard_map(
        per_device,
        mesh=mesh,
        in_specs=(
            P("tok", None), P("tok", None), P("tok", None), P("tok", None), P("tok", "chain"),
            P("chain", "tok", None), P("chain", None, "tok"), P("chain", "tok", None), P("chain", None, "tok"),
            P("chain"), P(),
        ),
        out_specs=(P("chain", "tok", None), P("chain", None, "tok")),
        check_vma=False,
    )
```

```python
import math, functools
import jax, jax.numpy as jnp
from jax import lax
from jax.experimental import pallas as pl
from jax.experimental.pallas import tpu as pltpu
HD=128; RANK=64
LOG2E=1.4426950408889634
f32=jnp.float32; bf16=jnp.bfloat16
NT=(((1,),(1,)),((),()))
NN=(((1,),(0,)),((),()))
TN=(((0,),(0,)),((),()))

def dot(a,b,dims):
    return lax.dot_general(a,b,dims,preferred_element_type=f32)

def attention_kernel(scale, nchain, group, pair, pos_ref, q_ref, do_ref, v_ref, base_ref, lr_ref, b_ref, lg_ref, rt_ref, acc_ref):
    T = q_ref.shape[0]
    nb = T // 128
    ss = 1.0 / math.sqrt(HD)
    step = pl.program_id(0)

    @pl.when(step == 0)
    def _():
        acc_ref[...] = jnp.zeros_like(acc_ref)

    per_head = HD // b_ref.shape[2]
    b = jnp.concatenate([b_ref[pos_ref[1 + step * per_head + i]] for i in range(per_head)], axis=1)
    b = [b[c * RANK:(c + 1) * RANK] for c in range(nchain)]
    lr = [lr_ref[:, c * RANK:(c + 1) * RANK] for c in range(nchain)]
    keys = [(base_ref[0].astype(f32) + scale * dot(lr[c], b[c], NN)).astype(bf16) for c in range(nchain)]
    keys = [jnp.concatenate([x[j * 128:(j + 1) * 128] for x in keys], axis=0) for j in range(nb)]
    row = lax.broadcasted_iota(jnp.int32, (128, 128), 0)
    col = lax.broadcasted_iota(jnp.int32, (128, 128), 1)
    future = row > col
    v = v_ref[...]
    kg = [jnp.zeros((nchain * 128, HD), f32) for _ in range(nb)]
    for h0 in range(0, group, pair):
        def heads(ref, j):
            return jnp.concatenate([ref[j * 128:, (h0 + h) * HD:(h0 + h + 1) * HD] for h in range(pair)], axis=0)

        qs = [heads(q_ref, j) for j in range(nb)]
        dp = [dot(v[j * 128:(j + 1) * 128], heads(do_ref, j), NT) for j in range(nb)]
        s = [dot(keys[j], qs[j], NT) for j in range(nb)]
        ds = [[[None] * (pair * (nb - j)) for _ in range(nchain)] for j in range(nb)]
        for h in range(pair):
            for c in range(nchain):
                for i in range(nb):
                    def at(x, j, c):
                        k = h * (nb - j) + i - j
                        return x[j][c * 128:(c + 1) * 128, k * 128:(k + 1) * 128]

                    blocks = [at(s, j, c) for j in range(i + 1)]
                    blocks[i] = jnp.where(future, -1e30, blocks[i])
                    top = jnp.max(functools.reduce(jnp.maximum, blocks), axis=0, keepdims=True)
                    e = [jnp.exp2((x - top) * (ss * LOG2E)) for x in blocks]
                    d = [at(dp, j, 0) for j in range(i + 1)]
                    r = 1.0 / jnp.sum(functools.reduce(jnp.add, e), axis=0, keepdims=True)
                    center = r * jnp.sum(functools.reduce(jnp.add, [x * y for x, y in zip(e, d)]), axis=0, keepdims=True)
                    for j in range(i + 1):
                        ds[j][c][h * (nb - j) + i - j] = ((e[j] * r) * (d[j] - center)).astype(bf16)
        for j in range(nb):
            dsj = jnp.concatenate([jnp.concatenate(x, axis=1) for x in ds[j]], axis=0)
            kg[j] = kg[j] + dot(dsj, qs[j], NN)
    for c in range(nchain):
        g = (jnp.concatenate([x[c * 128:(c + 1) * 128] for x in kg], axis=0) * ss).astype(bf16)
        acc_ref[:, c * RANK:(c + 1) * RANK] += dot(g, b[c], NT)
        rt_ref[0, c] = scale * dot(lr[c], g, TN)

    @pl.when(step == pl.num_programs(0) - 1)
    def _():
        lg_ref[...] = (scale * acc_ref[...]).astype(lg_ref.dtype)


def attention(pos, q, do, v, base, lr, b, scale):
    T, KW = v.shape
    nchain = lr.shape[1] // RANK
    KH, group = KW // HD, q.shape[1] // KW
    hp = base.shape[2] // HD
    grid = pltpu.PrefetchScalarGridSpec(
        num_scalar_prefetch=1, grid=(KH,),
        in_specs=[
            pl.BlockSpec((T, group * HD), lambda g, p: (0, g)),
            pl.BlockSpec((T, group * HD), lambda g, p: (0, g)),
            pl.BlockSpec((T, HD), lambda g, p: (0, g)),
            pl.BlockSpec((1, T, HD), lambda g, p: (p[0] ^ (g // hp), 0, g % hp)),
            pl.BlockSpec(lr.shape, lambda g, p: (0, 0)),
            pl.BlockSpec(b.shape, lambda g, p: (0, 0, 0)),
        ],
        out_specs=[
            pl.BlockSpec(lr.shape, lambda g, p: (0, 0)),
            pl.BlockSpec((1, nchain, RANK, HD), lambda g, p: (g, 0, 0, 0)),
        ],
        scratch_shapes=[pltpu.VMEM(lr.shape, f32)],
    )
    return pl.pallas_call(
        functools.partial(attention_kernel, scale, nchain, group, 4), grid_spec=grid,
        out_shape=[jax.ShapeDtypeStruct(lr.shape, bf16), jax.ShapeDtypeStruct((KH, nchain, RANK, HD), f32)],
        compiler_params=pltpu.CompilerParams(vmem_limit_bytes=28 * 1024 * 1024),
        cost_estimate=pl.CostEstimate(flops=10_000_000_000, bytes_accessed=20_000_000, transcendentals=T * T * 64 * nchain),
        name="attention",
    )(pos, q, do, v, base, lr, b)


from jax.sharding import PartitionSpec as P

STRIDE_LENGTH = 0.2


def gradient_kernel(own, nrank, pos_ref, x_ref, lg_ref, rt_ref, out_ref):
    g = dot(lg_ref[...], x_ref[...], TN)
    for c in range(nrank // RANK):
        out_ref[0, c] = jnp.concatenate([g[c * RANK:(c + 1) * RANK], rt_ref[0, c]], axis=1).astype(out_ref.dtype)


def gradients(pos, x, lg, rt, n, dtype):
    T, width = x.shape
    nrank = lg.shape[1]
    shards = 2 * n
    heads, nchain, _, kcols = rt.shape
    cols, kcols = width // shards, heads * kcols // shards
    if heads != shards:
        rt = rt.reshape(heads, nchain, RANK, -1, kcols).transpose(0, 3, 1, 2, 4).reshape(shards, nchain, RANK, kcols)
    grid = pltpu.PrefetchScalarGridSpec(
        num_scalar_prefetch=1, grid=(n,),
        in_specs=[
            pl.BlockSpec((T, cols), lambda i, p: (0, p[i])),
            pl.BlockSpec((T, nrank), lambda i, p: (0, 0)),
            pl.BlockSpec((1, nchain, RANK, kcols), lambda i, p: (p[i], 0, 0, 0)),
        ],
        out_specs=pl.BlockSpec((1, nchain, RANK, cols + kcols), lambda i, p: (i, 0, 0, 0)),
    )
    return pl.pallas_call(
        functools.partial(gradient_kernel, n, nrank), grid_spec=grid,
        out_shape=jax.ShapeDtypeStruct((n, nchain, RANK, cols + kcols), dtype),
        compiler_params=pltpu.CompilerParams(vmem_limit_bytes=24 * 1024 * 1024),
        cost_estimate=pl.CostEstimate(flops=T * width * nrank, bytes_accessed=3_000_000, transcendentals=0),
        name="gradients",
    )(pos, x, lg, rt)


def reorder_kernel(pos_ref, x_ref, out_ref):
    out_ref[...] = x_ref[...]


def reorder(pos, x, cols):
    T, width = x.shape
    grid = pltpu.PrefetchScalarGridSpec(
        num_scalar_prefetch=1, grid=(width // cols,),
        in_specs=[pl.BlockSpec((T, cols), lambda i, p: (0, p[i]))],
        out_specs=pl.BlockSpec((T, cols), lambda i, p: (0, i)),
    )
    return pl.pallas_call(
        reorder_kernel, grid_spec=grid, out_shape=jax.ShapeDtypeStruct(x.shape, x.dtype),
        compiler_params=pltpu.CompilerParams(vmem_limit_bytes=8 * 1024 * 1024),
        cost_estimate=pl.CostEstimate(flops=0, bytes_accessed=64 * T * width, transcendentals=0), name="reorder",
    )(pos, x)


def per_device(layer_activations, rotated_probes, attended_contents, attended_slope, locked_projection,
               first_multipliers, second_multipliers, first_jitter, second_jitter, chain_heats, donor_chain):
    T, width = layer_activations.shape
    scale = 1.0 / math.sqrt(width * RANK)
    nchain, arows, _ = first_multipliers.shape
    nc = lax.axis_size("chain")
    nt = lax.axis_size("tok")
    nz = nt // 2
    p = lax.axis_index("chain")
    t = lax.axis_index("tok")
    z, core = t // 2, t % 2

    def shift(x, k):
        return lax.ppermute(x, "tok", [(i, (i + 2 * k) % nt) for i in range(nt)])

    def swap_cores(x):
        return lax.ppermute(x, "tok", [(i, i ^ 1) for i in range(nt)])

    def exchange(x, k):
        return lax.ppermute(x, "chain", [(i, i ^ k) for i in range(nc)])

    source = lax.dynamic_slice_in_dim(donor_chain, p * nchain, nchain)

    def gather_slots(own):
        return [own] + [exchange(own, k) for k in range(1, nc)]

    def take_slots(parts, source):
        every = jnp.concatenate(parts)
        return jnp.concatenate([
            lax.dynamic_slice_in_dim(every, (source[j] // nchain ^ p) * nchain + source[j] % nchain, 1)
            for j in range(nchain)
        ])

    first = first_multipliers.transpose(0, 2, 1)
    kcols = second_multipliers.shape[2]
    nrank = nchain * RANK

    offsets = [0]
    for k in range(1, nz // 2):
        offsets += [-k, k]
    offsets.append(nz // 2)
    order = []
    for k in offsets:
        order += [(z + k) % nz * 2 + core, (z + k) % nz * 2 + 1 - core]

    def onward(shards, k):
        if k < nz // 2:
            up, down = (shards[-2], shards[-1]) if k > 1 else (shards[0], shards[0])
            return [shift(up, 1), shift(down, -1)]
        return [shift(shards[-2], 1)]

    w = [locked_projection]
    w += onward(w, 1)
    ab_own = jnp.concatenate([first, second_multipliers], axis=2).astype(bf16)
    ab = take_slots(gather_slots(ab_own), source).reshape(nrank, arows + kcols)
    heats, w, ab = lax.optimization_barrier((chain_heats, w, ab))
    up, down = [ab], [ab]
    for k in range(2, nz // 2 + 1):
        w += onward(w, k)
        up.append(shift(up[-1], 1))
    w_there = [swap_cores(x) for x in w[:-1]]
    heat = jnp.sqrt(2.0 * STRIDE_LENGTH * heats)[:, None, None]
    pre_a = (1.0 - STRIDE_LENGTH) * first + heat * first_jitter.transpose(0, 2, 1)
    pre_b = (1.0 - STRIDE_LENGTH) * second_multipliers + heat * second_jitter
    rest_own = jnp.concatenate([pre_a, pre_b], axis=2).astype(bf16)
    rest_own, w_there, order = lax.optimization_barrier((rest_own, w_there, jnp.stack(order).astype(jnp.int32)))
    x_ordered = reorder(order, layer_activations, arows)
    rest_parts = gather_slots(rest_own)
    w, up, w_there, x_ordered, down = lax.optimization_barrier((w, up, w_there, x_ordered, down))
    up.append(shift(up[-1], 1))
    for k in range(1, nz // 2):
        down.append(shift(down[-1], -1))
    def x_piece(s, theirs):
        return x_ordered[:, (2 * s + theirs) * arows:(2 * s + theirs + 1) * arows]

    def add(total, s, here, there, dims):
        for i, x in enumerate((here, there)):
            total = total + dot(x_piece(s, i), x, dims)
        return total

    w_there.append(swap_cores(w[-1]))
    plain = 0.0
    for s in range(nz):
        plain = add(plain, s, w[s], w_there[s], NN)
    plain = plain.astype(bf16)
    base = jnp.stack([plain] + [exchange(plain, k) for k in range(1, nc)])
    a = [ab]
    for k in range(1, nz // 2):
        a += [up[k], down[k]]
    a.append(up[-1])
    low_rank, b_low = 0.0, []
    for s in range(nz):
        if s == 2:
            base, a, low_rank = lax.optimization_barrier((base, a, low_rank))
        there = swap_cores(a[s])
        low_rank = add(low_rank, s, a[s][:, :arows], there[:, :arows], NT)
        b_low += [a[s][:, arows:], there[:, arows:]]
    low_rank = low_rank.astype(bf16)
    shards = jnp.arange(nt, dtype=jnp.int32)
    step_of = jnp.array([[k % nz for k in offsets].index(d) for d in range(nz)], jnp.int32)
    places = step_of[(shards // 2 - z) % nz] * 2 + (shards % 2 != core).astype(jnp.int32)
    pos = jnp.concatenate([p[None], places]).astype(jnp.int32)

    low_grad, right = attention(pos, rotated_probes, attended_slope, attended_contents, base, low_rank, jnp.stack(b_low), scale)

    low_grad, right, rest_parts = lax.optimization_barrier((low_grad, right, rest_parts))
    rest = take_slots(rest_parts, source)
    around = (z + jnp.arange(nz, dtype=jnp.int32)) % nz
    theirs = swap_cores(gradients(around * 2 + 1 - core, layer_activations, low_grad, right, nz, bf16))
    mine = gradients(around * 2 + core, layer_activations, low_grad, right, nz, f32)
    total = mine[0] + theirs[0]
    send = (mine[1:] + theirs[1:]).astype(bf16)
    for k in range(1, nz):
        total = total + shift(send[k - 1], k).astype(f32)
    new = rest.astype(f32) - STRIDE_LENGTH * total
    return new[:, :, :arows].transpose(0, 2, 1), new[:, :, arows:]


def solution(mesh):
    return jax.shard_map(
        per_device,
        mesh=mesh,
        in_specs=(
            P("tok", None), P("tok", None), P("tok", None), P("tok", None), P("tok", "chain"),
            P("chain", "tok", None), P("chain", None, "tok"), P("chain", "tok", None), P("chain", None, "tok"),
            P("chain"), P(),
        ),
        out_specs=(P("chain", "tok", None), P("chain", None, "tok")),
        check_vma=False,
    )
```

```python
import math, functools
import jax, jax.numpy as jnp
from jax import lax
from jax.experimental import pallas as pl
from jax.experimental.pallas import tpu as pltpu
HD=128; RANK=64
LOG2E=1.4426950408889634
f32=jnp.float32; bf16=jnp.bfloat16
NT=(((1,),(1,)),((),()))
NN=(((1,),(0,)),((),()))
TN=(((0,),(0,)),((),()))

def dot(a,b,dims):
    return lax.dot_general(a,b,dims,preferred_element_type=f32)

def attention_kernel(scale, nchain, group, pair, pos_ref, q_ref, do_ref, v_ref, base_ref, lr_ref, b_ref, lg_ref, rt_ref, acc_ref):
    T = q_ref.shape[0]
    nb = T // 128
    ss = 1.0 / math.sqrt(HD)
    step = pl.program_id(0)

    @pl.when(step == 0)
    def _():
        acc_ref[...] = jnp.zeros_like(acc_ref)

    per_head = HD // b_ref.shape[2]
    b = jnp.concatenate([b_ref[pos_ref[1 + step * per_head + i]] for i in range(per_head)], axis=1)
    b = [b[c * RANK:(c + 1) * RANK] for c in range(nchain)]
    lr = [lr_ref[:, c * RANK:(c + 1) * RANK] for c in range(nchain)]
    keys = [(base_ref[0].astype(f32) + scale * dot(lr[c], b[c], NN)).astype(bf16) for c in range(nchain)]
    keys = [jnp.concatenate([x[j * 128:(j + 1) * 128] for x in keys], axis=0) for j in range(nb)]
    row = lax.broadcasted_iota(jnp.int32, (128, 128), 0)
    col = lax.broadcasted_iota(jnp.int32, (128, 128), 1)
    future = row > col
    v = v_ref[...]
    kg = [jnp.zeros((nchain * 128, HD), f32) for _ in range(nb)]
    for h0 in range(0, group, pair):
        def heads(ref, j):
            return jnp.concatenate([ref[j * 128:, (h0 + h) * HD:(h0 + h + 1) * HD] for h in range(pair)], axis=0)

        qs = [heads(q_ref, j) for j in range(nb)]
        dp = [dot(v[j * 128:(j + 1) * 128], heads(do_ref, j), NT) for j in range(nb)]
        s = [dot(keys[j], qs[j], NT) for j in range(nb)]
        ds = [[[None] * (pair * (nb - j)) for _ in range(nchain)] for j in range(nb)]
        for h in range(pair):
            for c in range(nchain):
                for i in range(nb):
                    def at(x, j, c):
                        k = h * (nb - j) + i - j
                        return x[j][c * 128:(c + 1) * 128, k * 128:(k + 1) * 128]

                    blocks = [at(s, j, c) for j in range(i + 1)]
                    blocks[i] = jnp.where(future, -1e30, blocks[i])
                    top = jnp.max(functools.reduce(jnp.maximum, blocks), axis=0, keepdims=True)
                    e = [jnp.exp2((x - top) * (ss * LOG2E)) for x in blocks]
                    d = [at(dp, j, 0) for j in range(i + 1)]
                    r = 1.0 / jnp.sum(functools.reduce(jnp.add, e), axis=0, keepdims=True)
                    center = r * jnp.sum(functools.reduce(jnp.add, [x * y for x, y in zip(e, d)]), axis=0, keepdims=True)
                    for j in range(i + 1):
                        ds[j][c][h * (nb - j) + i - j] = ((e[j] * r) * (d[j] - center)).astype(bf16)
        for j in range(nb):
            dsj = jnp.concatenate([jnp.concatenate(x, axis=1) for x in ds[j]], axis=0)
            kg[j] = kg[j] + dot(dsj, qs[j], NN)
    for c in range(nchain):
        g = (jnp.concatenate([x[c * 128:(c + 1) * 128] for x in kg], axis=0) * ss).astype(bf16)
        acc_ref[:, c * RANK:(c + 1) * RANK] += dot(g, b[c], NT)
        rt_ref[0, c] = scale * dot(lr[c], g, TN)

    @pl.when(step == pl.num_programs(0) - 1)
    def _():
        lg_ref[...] = (scale * acc_ref[...]).astype(lg_ref.dtype)


def attention(pos, q, do, v, base, lr, b, scale, pair=4):
    T, KW = v.shape
    nchain = lr.shape[1] // RANK
    KH, group = KW // HD, q.shape[1] // KW
    hp = base.shape[2] // HD
    grid = pltpu.PrefetchScalarGridSpec(
        num_scalar_prefetch=1, grid=(KH,),
        in_specs=[
            pl.BlockSpec((T, group * HD), lambda g, p: (0, g)),
            pl.BlockSpec((T, group * HD), lambda g, p: (0, g)),
            pl.BlockSpec((T, HD), lambda g, p: (0, g)),
            pl.BlockSpec((1, T, HD), lambda g, p: (p[0] ^ (g // hp), 0, g % hp)),
            pl.BlockSpec(lr.shape, lambda g, p: (0, 0)),
            pl.BlockSpec(b.shape, lambda g, p: (0, 0, 0)),
        ],
        out_specs=[
            pl.BlockSpec(lr.shape, lambda g, p: (0, 0)),
            pl.BlockSpec((1, nchain, RANK, HD), lambda g, p: (g, 0, 0, 0)),
        ],
        scratch_shapes=[pltpu.VMEM(lr.shape, f32)],
    )
    return pl.pallas_call(
        functools.partial(attention_kernel, scale, nchain, group, pair), grid_spec=grid,
        out_shape=[jax.ShapeDtypeStruct(lr.shape, bf16), jax.ShapeDtypeStruct((KH, nchain, RANK, HD), f32)],
        compiler_params=pltpu.CompilerParams(vmem_limit_bytes=28 * 1024 * 1024),
        cost_estimate=pl.CostEstimate(flops=10_000_000_000, bytes_accessed=20_000_000, transcendentals=T * T * 64 * nchain),
        name="attention",
    )(pos, q, do, v, base, lr, b)


from jax.sharding import PartitionSpec as P

STRIDE_LENGTH = 0.2


def gradient_kernel(own, nrank, pos_ref, x_ref, lg_ref, rt_ref, out_ref):
    g = dot(lg_ref[...], x_ref[...], TN)
    for c in range(nrank // RANK):
        out_ref[0, c] = jnp.concatenate([g[c * RANK:(c + 1) * RANK], rt_ref[0, c]], axis=1).astype(out_ref.dtype)


def gradients(pos, x, lg, rt, n, dtype):
    T, width = x.shape
    nrank = lg.shape[1]
    shards = 2 * n
    heads, nchain, _, kcols = rt.shape
    cols, kcols = width // shards, heads * kcols // shards
    if heads != shards:
        rt = rt.reshape(heads, nchain, RANK, -1, kcols).transpose(0, 3, 1, 2, 4).reshape(shards, nchain, RANK, kcols)
    grid = pltpu.PrefetchScalarGridSpec(
        num_scalar_prefetch=1, grid=(n,),
        in_specs=[
            pl.BlockSpec((T, cols), lambda i, p: (0, p[i])),
            pl.BlockSpec((T, nrank), lambda i, p: (0, 0)),
            pl.BlockSpec((1, nchain, RANK, kcols), lambda i, p: (p[i], 0, 0, 0)),
        ],
        out_specs=pl.BlockSpec((1, nchain, RANK, cols + kcols), lambda i, p: (i, 0, 0, 0)),
    )
    return pl.pallas_call(
        functools.partial(gradient_kernel, n, nrank), grid_spec=grid,
        out_shape=jax.ShapeDtypeStruct((n, nchain, RANK, cols + kcols), dtype),
        compiler_params=pltpu.CompilerParams(vmem_limit_bytes=24 * 1024 * 1024),
        cost_estimate=pl.CostEstimate(flops=T * width * nrank, bytes_accessed=3_000_000, transcendentals=0),
        name="gradients",
    )(pos, x, lg, rt)


def reorder_kernel(pos_ref, x_ref, out_ref):
    out_ref[...] = x_ref[...]


def reorder(pos, x, cols):
    T, width = x.shape
    grid = pltpu.PrefetchScalarGridSpec(
        num_scalar_prefetch=1, grid=(width // cols,),
        in_specs=[pl.BlockSpec((T, cols), lambda i, p: (0, p[i]))],
        out_specs=pl.BlockSpec((T, cols), lambda i, p: (0, i)),
    )
    return pl.pallas_call(
        reorder_kernel, grid_spec=grid, out_shape=jax.ShapeDtypeStruct(x.shape, x.dtype),
        compiler_params=pltpu.CompilerParams(vmem_limit_bytes=8 * 1024 * 1024),
        cost_estimate=pl.CostEstimate(flops=0, bytes_accessed=64 * T * width, transcendentals=0), name="reorder",
    )(pos, x)


def per_device(layer_activations, rotated_probes, attended_contents, attended_slope, locked_projection,
               first_multipliers, second_multipliers, first_jitter, second_jitter, chain_heats, donor_chain):
    T, width = layer_activations.shape
    scale = 1.0 / math.sqrt(width * RANK)
    nchain, arows, _ = first_multipliers.shape
    nc = lax.axis_size("chain")
    nt = lax.axis_size("tok")
    nz = nt // 2
    p = lax.axis_index("chain")
    t = lax.axis_index("tok")
    z, core = t // 2, t % 2

    def shift(x, k):
        return lax.ppermute(x, "tok", [(i, (i + 2 * k) % nt) for i in range(nt)])

    def swap_cores(x):
        return lax.ppermute(x, "tok", [(i, i ^ 1) for i in range(nt)])

    def exchange(x, k):
        return lax.ppermute(x, "chain", [(i, i ^ k) for i in range(nc)])

    source = lax.dynamic_slice_in_dim(donor_chain, p * nchain, nchain)

    def gather_slots(own):
        return [own] + [exchange(own, k) for k in range(1, nc)]

    def take_slots(parts, source):
        every = jnp.concatenate(parts)
        return jnp.concatenate([
            lax.dynamic_slice_in_dim(every, (source[j] // nchain ^ p) * nchain + source[j] % nchain, 1)
            for j in range(nchain)
        ])

    first = first_multipliers.transpose(0, 2, 1)
    kcols = second_multipliers.shape[2]
    nrank = nchain * RANK

    offsets = [0]
    for k in range(1, nz // 2):
        offsets += [-k, k]
    offsets.append(nz // 2)
    order = []
    for k in offsets:
        order += [(z + k) % nz * 2 + core, (z + k) % nz * 2 + 1 - core]

    def onward(shards, k):
        if k < nz // 2:
            up, down = (shards[-2], shards[-1]) if k > 1 else (shards[0], shards[0])
            return [shift(up, 1), shift(down, -1)]
        return [shift(shards[-2], 1)]

    w = [locked_projection]
    w += onward(w, 1)
    ab_own = jnp.concatenate([first, second_multipliers], axis=2).astype(bf16)
    ab = take_slots(gather_slots(ab_own), source).reshape(nrank, arows + kcols)
    heats, w, ab = lax.optimization_barrier((chain_heats, w, ab))
    up, down = [ab], [ab]
    for k in range(2, nz // 2 + 1):
        w += onward(w, k)
        up.append(shift(up[-1], 1))
    w_there = [swap_cores(x) for x in w[:-1]]
    heat = jnp.sqrt(2.0 * STRIDE_LENGTH * heats)[:, None, None]
    pre_a = (1.0 - STRIDE_LENGTH) * first + heat * first_jitter.transpose(0, 2, 1)
    pre_b = (1.0 - STRIDE_LENGTH) * second_multipliers + heat * second_jitter
    rest_own = jnp.concatenate([pre_a, pre_b], axis=2).astype(bf16)
    rest_own, w_there, order = lax.optimization_barrier((rest_own, w_there, jnp.stack(order).astype(jnp.int32)))
    x_ordered = reorder(order, layer_activations, arows)

    def x_piece(s, theirs):
        return x_ordered[:, (2 * s + theirs) * arows:(2 * s + theirs + 1) * arows]

    def add(total, s, here, there, dims):
        for i, x in enumerate((here, there)):
            total = total + dot(x_piece(s, i), x, dims)
        return total

    plain = 0.0
    for s in range(nz - 1):
        plain = add(plain, s, w[s], w_there[s], NN)
    rest_parts = gather_slots(rest_own)
    w[-1], up, w_there, down, rest_parts = lax.optimization_barrier((w[-1], up, w_there, down, rest_parts))
    up.append(shift(up[-1], 1))
    for k in range(1, nz // 2):
        down.append(shift(down[-1], -1))
    plain = add(plain, nz - 1, w[-1], swap_cores(w[-1]), NN).astype(bf16)
    base = jnp.stack([plain] + [exchange(plain, k) for k in range(1, nc)])
    a = [ab]
    for k in range(1, nz // 2):
        a += [up[k], down[k]]
    a.append(up[-1])
    low_rank, b_low = 0.0, []
    for s in range(nz):
        if s == 2:
            base, a, low_rank = lax.optimization_barrier((base, a, low_rank))
        there = swap_cores(a[s])
        low_rank = add(low_rank, s, a[s][:, :arows], there[:, :arows], NT)
        b_low += [a[s][:, arows:], there[:, arows:]]
    low_rank = low_rank.astype(bf16)
    shards = jnp.arange(nt, dtype=jnp.int32)
    step_of = jnp.array([[k % nz for k in offsets].index(d) for d in range(nz)], jnp.int32)
    places = step_of[(shards // 2 - z) % nz] * 2 + (shards % 2 != core).astype(jnp.int32)
    pos = jnp.concatenate([p[None], places]).astype(jnp.int32)

    low_grad, right = attention(pos, rotated_probes, attended_slope, attended_contents, base, low_rank, jnp.stack(b_low), scale)

    low_grad, right, rest_parts = lax.optimization_barrier((low_grad, right, rest_parts))
    rest = take_slots(rest_parts, source)
    around = (z + jnp.arange(nz, dtype=jnp.int32)) % nz
    theirs = swap_cores(gradients(around * 2 + 1 - core, layer_activations, low_grad, right, nz, bf16))
    mine = gradients(around * 2 + core, layer_activations, low_grad, right, nz, f32)
    total = mine[0] + theirs[0]
    send = (mine[1:] + theirs[1:]).astype(bf16)
    for k in range(1, nz):
        total = total + shift(send[k - 1], k).astype(f32)
    new = rest.astype(f32) - STRIDE_LENGTH * total
    return new[:, :, :arows].transpose(0, 2, 1), new[:, :, arows:]


def solution(mesh):
    return jax.shard_map(
        per_device,
        mesh=mesh,
        in_specs=(
            P("tok", None), P("tok", None), P("tok", None), P("tok", None), P("tok", "chain"),
            P("chain", "tok", None), P("chain", None, "tok"), P("chain", "tok", None), P("chain", None, "tok"),
            P("chain"), P(),
        ),
        out_specs=(P("chain", "tok", None), P("chain", None, "tok")),
        check_vma=False,
    )
```

```python
import math, functools
import jax, jax.numpy as jnp
from jax import lax
from jax.experimental import pallas as pl
from jax.experimental.pallas import tpu as pltpu
HD=128; RANK=64
LOG2E=1.4426950408889634
f32=jnp.float32; bf16=jnp.bfloat16
NT=(((1,),(1,)),((),()))
NN=(((1,),(0,)),((),()))
TN=(((0,),(0,)),((),()))

def dot(a,b,dims):
    return lax.dot_general(a,b,dims,preferred_element_type=f32)

def attention_kernel(scale, nchain, group, pair, pos_ref, q_ref, do_ref, v_ref, base_ref, lr_ref, b_ref, lg_ref, rt_ref, acc_ref):
    T = q_ref.shape[0]
    nb = T // 128
    ss = 1.0 / math.sqrt(HD)
    step = pl.program_id(0)

    @pl.when(step == 0)
    def _():
        acc_ref[...] = jnp.zeros_like(acc_ref)

    per_head = HD // b_ref.shape[2]
    row = lax.broadcasted_iota(jnp.int32, (128, 128), 0)
    col = lax.broadcasted_iota(jnp.int32, (128, 128), 1)
    future = row > col
    heads_here = v_ref.shape[1] // HD
    for n in range(heads_here):
        b = jnp.concatenate([b_ref[pos_ref[1 + (step * heads_here + n) * per_head + i]] for i in range(per_head)], axis=1)
        b = [b[c * RANK:(c + 1) * RANK] for c in range(nchain)]
        lr = [lr_ref[:, c * RANK:(c + 1) * RANK] for c in range(nchain)]
        keys = [(base_ref[0, :, n * HD:(n + 1) * HD].astype(f32) + scale * dot(lr[c], b[c], NN)).astype(bf16) for c in range(nchain)]
        keys = [jnp.concatenate([x[j * 128:(j + 1) * 128] for x in keys], axis=0) for j in range(nb)]
        v = v_ref[:, n * HD:(n + 1) * HD]
        kg = [jnp.zeros((nchain * 128, HD), f32) for _ in range(nb)]
        for h0 in range(0, group, pair):
            def heads(ref, j):
                return jnp.concatenate([ref[j * 128:, (n * group + h0 + h) * HD:(n * group + h0 + h + 1) * HD] for h in range(pair)], axis=0)

            qs = [heads(q_ref, j) for j in range(nb)]
            dp = [dot(v[j * 128:(j + 1) * 128], heads(do_ref, j), NT) for j in range(nb)]
            s = [dot(keys[j], qs[j], NT) for j in range(nb)]
            ds = [[[None] * (pair * (nb - j)) for _ in range(nchain)] for j in range(nb)]
            for h in range(pair):
                for c in range(nchain):
                    for i in range(nb):
                        def at(x, j, c):
                            k = h * (nb - j) + i - j
                            return x[j][c * 128:(c + 1) * 128, k * 128:(k + 1) * 128]

                        blocks = [at(s, j, c) for j in range(i + 1)]
                        blocks[i] = jnp.where(future, -1e30, blocks[i])
                        top = jnp.max(functools.reduce(jnp.maximum, blocks), axis=0, keepdims=True)
                        e = [jnp.exp2((x - top) * (ss * LOG2E)) for x in blocks]
                        d = [at(dp, j, 0) for j in range(i + 1)]
                        r = 1.0 / jnp.sum(functools.reduce(jnp.add, e), axis=0, keepdims=True)
                        center = r * jnp.sum(functools.reduce(jnp.add, [x * y for x, y in zip(e, d)]), axis=0, keepdims=True)
                        for j in range(i + 1):
                            ds[j][c][h * (nb - j) + i - j] = ((e[j] * r) * (d[j] - center)).astype(bf16)
            for j in range(nb):
                dsj = jnp.concatenate([jnp.concatenate(x, axis=1) for x in ds[j]], axis=0)
                kg[j] = kg[j] + dot(dsj, qs[j], NN)
        for c in range(nchain):
            g = (jnp.concatenate([x[c * 128:(c + 1) * 128] for x in kg], axis=0) * ss).astype(bf16)
            acc_ref[:, c * RANK:(c + 1) * RANK] += dot(g, b[c], NT)
            rt_ref[n, c] = scale * dot(lr[c], g, TN)

    @pl.when(step == pl.num_programs(0) - 1)
    def _():
        lg_ref[...] = (scale * acc_ref[...]).astype(lg_ref.dtype)


def attention(pos, q, do, v, base, lr, b, scale, pair=4):
    T, KW = v.shape
    nchain = lr.shape[1] // RANK
    KH, group = KW // HD, q.shape[1] // KW
    hp = base.shape[2] // HD
    grid = pltpu.PrefetchScalarGridSpec(
        num_scalar_prefetch=1, grid=(KH // hp,),
        in_specs=[
            pl.BlockSpec((T, hp * group * HD), lambda g, p: (0, g)),
            pl.BlockSpec((T, hp * group * HD), lambda g, p: (0, g)),
            pl.BlockSpec((T, hp * HD), lambda g, p: (0, g)),
            pl.BlockSpec((1, T, hp * HD), lambda g, p: (p[0] ^ g, 0, 0)),
            pl.BlockSpec(lr.shape, lambda g, p: (0, 0)),
            pl.BlockSpec(b.shape, lambda g, p: (0, 0, 0)),
        ],
        out_specs=[
            pl.BlockSpec(lr.shape, lambda g, p: (0, 0)),
            pl.BlockSpec((hp, nchain, RANK, HD), lambda g, p: (g, 0, 0, 0)),
        ],
        scratch_shapes=[pltpu.VMEM(lr.shape, f32)],
    )
    return pl.pallas_call(
        functools.partial(attention_kernel, scale, nchain, group, pair), grid_spec=grid,
        out_shape=[jax.ShapeDtypeStruct(lr.shape, bf16), jax.ShapeDtypeStruct((KH, nchain, RANK, HD), f32)],
        compiler_params=pltpu.CompilerParams(vmem_limit_bytes=40 * 1024 * 1024),
        cost_estimate=pl.CostEstimate(flops=10_000_000_000, bytes_accessed=20_000_000, transcendentals=T * T * 64 * nchain),
        name="attention",
    )(pos, q, do, v, base, lr, b)


from jax.sharding import PartitionSpec as P

STRIDE_LENGTH = 0.2


def gradient_kernel(own, nrank, pos_ref, x_ref, lg_ref, rt_ref, out_ref):
    g = dot(lg_ref[...], x_ref[...], TN)
    for c in range(nrank // RANK):
        out_ref[0, c] = jnp.concatenate([g[c * RANK:(c + 1) * RANK], rt_ref[0, c]], axis=1).astype(out_ref.dtype)


def gradients(pos, x, lg, rt, n, dtype):
    T, width = x.shape
    nrank = lg.shape[1]
    shards = 2 * n
    heads, nchain, _, kcols = rt.shape
    cols, kcols = width // shards, heads * kcols // shards
    if heads != shards:
        rt = rt.reshape(heads, nchain, RANK, -1, kcols).transpose(0, 3, 1, 2, 4).reshape(shards, nchain, RANK, kcols)
    grid = pltpu.PrefetchScalarGridSpec(
        num_scalar_prefetch=1, grid=(n,),
        in_specs=[
            pl.BlockSpec((T, cols), lambda i, p: (0, p[i])),
            pl.BlockSpec((T, nrank), lambda i, p: (0, 0)),
            pl.BlockSpec((1, nchain, RANK, kcols), lambda i, p: (p[i], 0, 0, 0)),
        ],
        out_specs=pl.BlockSpec((1, nchain, RANK, cols + kcols), lambda i, p: (i, 0, 0, 0)),
    )
    return pl.pallas_call(
        functools.partial(gradient_kernel, n, nrank), grid_spec=grid,
        out_shape=jax.ShapeDtypeStruct((n, nchain, RANK, cols + kcols), dtype),
        compiler_params=pltpu.CompilerParams(vmem_limit_bytes=24 * 1024 * 1024),
        cost_estimate=pl.CostEstimate(flops=T * width * nrank, bytes_accessed=3_000_000, transcendentals=0),
        name="gradients",
    )(pos, x, lg, rt)


def reorder_kernel(pos_ref, x_ref, out_ref):
    out_ref[...] = x_ref[...]


def reorder(pos, x, cols):
    T, width = x.shape
    grid = pltpu.PrefetchScalarGridSpec(
        num_scalar_prefetch=1, grid=(width // cols,),
        in_specs=[pl.BlockSpec((T, cols), lambda i, p: (0, p[i]))],
        out_specs=pl.BlockSpec((T, cols), lambda i, p: (0, i)),
    )
    return pl.pallas_call(
        reorder_kernel, grid_spec=grid, out_shape=jax.ShapeDtypeStruct(x.shape, x.dtype),
        compiler_params=pltpu.CompilerParams(vmem_limit_bytes=8 * 1024 * 1024),
        cost_estimate=pl.CostEstimate(flops=0, bytes_accessed=64 * T * width, transcendentals=0), name="reorder",
    )(pos, x)


def per_device(layer_activations, rotated_probes, attended_contents, attended_slope, locked_projection,
               first_multipliers, second_multipliers, first_jitter, second_jitter, chain_heats, donor_chain):
    T, width = layer_activations.shape
    scale = 1.0 / math.sqrt(width * RANK)
    nchain, arows, _ = first_multipliers.shape
    nc = lax.axis_size("chain")
    nt = lax.axis_size("tok")
    nz = nt // 2
    p = lax.axis_index("chain")
    t = lax.axis_index("tok")
    z, core = t // 2, t % 2

    def shift(x, k):
        return lax.ppermute(x, "tok", [(i, (i + 2 * k) % nt) for i in range(nt)])

    def swap_cores(x):
        return lax.ppermute(x, "tok", [(i, i ^ 1) for i in range(nt)])

    def exchange(x, k):
        return lax.ppermute(x, "chain", [(i, i ^ k) for i in range(nc)])

    source = lax.dynamic_slice_in_dim(donor_chain, p * nchain, nchain)

    def gather_slots(own):
        return [own] + [exchange(own, k) for k in range(1, nc)]

    def take_slots(parts, source):
        every = jnp.concatenate(parts)
        return jnp.concatenate([
            lax.dynamic_slice_in_dim(every, (source[j] // nchain ^ p) * nchain + source[j] % nchain, 1)
            for j in range(nchain)
        ])

    first = first_multipliers.transpose(0, 2, 1)
    kcols = second_multipliers.shape[2]
    nrank = nchain * RANK

    offsets = [0]
    for k in range(1, nz // 2):
        offsets += [-k, k]
    offsets.append(nz // 2)
    order = []
    for k in offsets:
        order += [(z + k) % nz * 2 + core, (z + k) % nz * 2 + 1 - core]

    def onward(shards, k):
        if k < nz // 2:
            up, down = (shards[-2], shards[-1]) if k > 1 else (shards[0], shards[0])
            return [shift(up, 1), shift(down, -1)]
        return [shift(shards[-2], 1)]

    w = [locked_projection]
    w += onward(w, 1)
    ab_own = jnp.concatenate([first, second_multipliers], axis=2).astype(bf16)
    ab = take_slots(gather_slots(ab_own), source).reshape(nrank, arows + kcols)
    heats, w, ab = lax.optimization_barrier((chain_heats, w, ab))
    up, down = [ab], [ab]
    for k in range(2, nz // 2 + 1):
        w += onward(w, k)
        up.append(shift(up[-1], 1))
    w_there = [swap_cores(x) for x in w[:-1]]
    heat = jnp.sqrt(2.0 * STRIDE_LENGTH * heats)[:, None, None]
    pre_a = (1.0 - STRIDE_LENGTH) * first + heat * first_jitter.transpose(0, 2, 1)
    pre_b = (1.0 - STRIDE_LENGTH) * second_multipliers + heat * second_jitter
    rest_own = jnp.concatenate([pre_a, pre_b], axis=2).astype(bf16)
    rest_own, w_there, order = lax.optimization_barrier((rest_own, w_there, jnp.stack(order).astype(jnp.int32)))
    x_ordered = reorder(order, layer_activations, arows)

    def x_piece(s, theirs):
        return x_ordered[:, (2 * s + theirs) * arows:(2 * s + theirs + 1) * arows]

    def add(total, s, here, there, dims):
        for i, x in enumerate((here, there)):
            total = total + dot(x_piece(s, i), x, dims)
        return total

    plain = 0.0
    for s in range(nz - 1):
        plain = add(plain, s, w[s], w_there[s], NN)
    rest_parts = gather_slots(rest_own)
    w[-1], up, w_there, down, rest_parts = lax.optimization_barrier((w[-1], up, w_there, down, rest_parts))
    up.append(shift(up[-1], 1))
    for k in range(1, nz // 2):
        down.append(shift(down[-1], -1))
    plain = add(plain, nz - 1, w[-1], swap_cores(w[-1]), NN).astype(bf16)
    base = jnp.stack([plain] + [exchange(plain, k) for k in range(1, nc)])
    a = [ab]
    for k in range(1, nz // 2):
        a += [up[k], down[k]]
    a.append(up[-1])
    low_rank, b_low = 0.0, []
    for s in range(nz):
        if s == 2:
            base, a, low_rank = lax.optimization_barrier((base, a, low_rank))
        there = swap_cores(a[s])
        low_rank = add(low_rank, s, a[s][:, :arows], there[:, :arows], NT)
        b_low += [a[s][:, arows:], there[:, arows:]]
    low_rank = low_rank.astype(bf16)
    shards = jnp.arange(nt, dtype=jnp.int32)
    step_of = jnp.array([[k % nz for k in offsets].index(d) for d in range(nz)], jnp.int32)
    places = step_of[(shards // 2 - z) % nz] * 2 + (shards % 2 != core).astype(jnp.int32)
    pos = jnp.concatenate([p[None], places]).astype(jnp.int32)

    low_grad, right = attention(pos, rotated_probes, attended_slope, attended_contents, base, low_rank, jnp.stack(b_low), scale)

    low_grad, right, rest_parts = lax.optimization_barrier((low_grad, right, rest_parts))
    rest = take_slots(rest_parts, source)
    around = (z + jnp.arange(nz, dtype=jnp.int32)) % nz
    theirs = swap_cores(gradients(around * 2 + 1 - core, layer_activations, low_grad, right, nz, bf16))
    mine = gradients(around * 2 + core, layer_activations, low_grad, right, nz, f32)
    total = mine[0] + theirs[0]
    send = (mine[1:] + theirs[1:]).astype(bf16)
    for k in sorted(range(1, nz), key=lambda k: min(k, nz - k)):
        total = total + shift(send[k - 1], k).astype(f32)
    new = rest.astype(f32) - STRIDE_LENGTH * total
    return new[:, :, :arows].transpose(0, 2, 1), new[:, :, arows:]


def solution(mesh):
    return jax.shard_map(
        per_device,
        mesh=mesh,
        in_specs=(
            P("tok", None), P("tok", None), P("tok", None), P("tok", None), P("tok", "chain"),
            P("chain", "tok", None), P("chain", None, "tok"), P("chain", "tok", None), P("chain", None, "tok"),
            P("chain"), P(),
        ),
        out_specs=(P("chain", "tok", None), P("chain", None, "tok")),
        check_vma=False,
    )
```

```python
import math, functools
import jax, jax.numpy as jnp
from jax import lax
from jax.experimental import pallas as pl
from jax.experimental.pallas import tpu as pltpu
HD=128; RANK=64
LOG2E=1.4426950408889634
f32=jnp.float32; bf16=jnp.bfloat16
NT=(((1,),(1,)),((),()))
NN=(((1,),(0,)),((),()))
TN=(((0,),(0,)),((),()))

def dot(a,b,dims):
    return lax.dot_general(a,b,dims,preferred_element_type=f32)

def attention_kernel(scale, nchain, group, pair, pos_ref, q_ref, do_ref, v_ref, base_ref, lr_ref, b_ref, lg_ref, rt_ref, acc_ref):
    T = q_ref.shape[0]
    nb = T // 128
    ss = 1.0 / math.sqrt(HD)
    step = pl.program_id(0)

    @pl.when(step == 0)
    def _():
        acc_ref[...] = jnp.zeros_like(acc_ref)

    per_head = HD // b_ref.shape[2]
    row = lax.broadcasted_iota(jnp.int32, (128, 128), 0)
    col = lax.broadcasted_iota(jnp.int32, (128, 128), 1)
    future = row > col
    heads_here = v_ref.shape[1] // HD
    for n in range(heads_here):
        b = jnp.concatenate([b_ref[pos_ref[1 + (step * heads_here + n) * per_head + i]] for i in range(per_head)], axis=1)
        b = [b[c * RANK:(c + 1) * RANK] for c in range(nchain)]
        lr = [lr_ref[:, c * RANK:(c + 1) * RANK] for c in range(nchain)]
        keys = [(base_ref[0, :, n * HD:(n + 1) * HD].astype(f32) + scale * dot(lr[c], b[c], NN)).astype(bf16) for c in range(nchain)]
        keys = [jnp.concatenate([x[j * 128:(j + 1) * 128] for x in keys], axis=0) for j in range(nb)]
        v = v_ref[:, n * HD:(n + 1) * HD]
        kg = [jnp.zeros((nchain * 128, HD), f32) for _ in range(nb)]
        for h0 in range(0, group, pair):
            def heads(ref, j):
                return jnp.concatenate([ref[j * 128:, (n * group + h0 + h) * HD:(n * group + h0 + h + 1) * HD] for h in range(pair)], axis=0)

            qs = [heads(q_ref, j) for j in range(nb)]
            dp = [dot(v[j * 128:(j + 1) * 128], heads(do_ref, j), NT) for j in range(nb)]
            s = [dot(keys[j], qs[j], NT) for j in range(nb)]
            ds = [[[None] * (pair * (nb - j)) for _ in range(nchain)] for j in range(nb)]
            for h in range(pair):
                for c in range(nchain):
                    for i in range(nb):
                        def at(x, j, c):
                            k = h * (nb - j) + i - j
                            return x[j][c * 128:(c + 1) * 128, k * 128:(k + 1) * 128]

                        blocks = [at(s, j, c) for j in range(i + 1)]
                        blocks[i] = jnp.where(future, -1e30, blocks[i])
                        top = jnp.max(functools.reduce(jnp.maximum, blocks), axis=0, keepdims=True)
                        e = [jnp.exp2((x - top) * (ss * LOG2E)) for x in blocks]
                        d = [at(dp, j, 0) for j in range(i + 1)]
                        r = 1.0 / jnp.sum(functools.reduce(jnp.add, e), axis=0, keepdims=True)
                        center = r * jnp.sum(functools.reduce(jnp.add, [x * y for x, y in zip(e, d)]), axis=0, keepdims=True)
                        for j in range(i + 1):
                            ds[j][c][h * (nb - j) + i - j] = ((e[j] * r) * (d[j] - center)).astype(bf16)
            for j in range(nb):
                dsj = jnp.concatenate([jnp.concatenate(x, axis=1) for x in ds[j]], axis=0)
                kg[j] = kg[j] + dot(dsj, qs[j], NN)
        for c in range(nchain):
            g = (jnp.concatenate([x[c * 128:(c + 1) * 128] for x in kg], axis=0) * ss).astype(bf16)
            acc_ref[:, c * RANK:(c + 1) * RANK] += dot(g, b[c], NT)
            rt_ref[n, c] = scale * dot(lr[c], g, TN)

    @pl.when(step == pl.num_programs(0) - 1)
    def _():
        lg_ref[...] = (scale * acc_ref[...]).astype(lg_ref.dtype)


def attention(pos, q, do, v, base, lr, b, scale, pair=4):
    T, KW = v.shape
    nchain = lr.shape[1] // RANK
    KH, group = KW // HD, q.shape[1] // KW
    hp = base.shape[2] // HD
    grid = pltpu.PrefetchScalarGridSpec(
        num_scalar_prefetch=1, grid=(KH // hp,),
        in_specs=[
            pl.BlockSpec((T, hp * group * HD), lambda g, p: (0, g)),
            pl.BlockSpec((T, hp * group * HD), lambda g, p: (0, g)),
            pl.BlockSpec((T, hp * HD), lambda g, p: (0, g)),
            pl.BlockSpec((1, T, hp * HD), lambda g, p: (p[0] ^ g, 0, 0)),
            pl.BlockSpec(lr.shape, lambda g, p: (0, 0)),
            pl.BlockSpec(b.shape, lambda g, p: (0, 0, 0)),
        ],
        out_specs=[
            pl.BlockSpec(lr.shape, lambda g, p: (0, 0)),
            pl.BlockSpec((hp, nchain, RANK, HD), lambda g, p: (g, 0, 0, 0)),
        ],
        scratch_shapes=[pltpu.VMEM(lr.shape, f32)],
    )
    return pl.pallas_call(
        functools.partial(attention_kernel, scale, nchain, group, pair), grid_spec=grid,
        out_shape=[jax.ShapeDtypeStruct(lr.shape, bf16), jax.ShapeDtypeStruct((KH, nchain, RANK, HD), f32)],
        compiler_params=pltpu.CompilerParams(vmem_limit_bytes=40 * 1024 * 1024),
        cost_estimate=pl.CostEstimate(flops=10_000_000_000, bytes_accessed=20_000_000, transcendentals=T * T * 64 * nchain),
        name="attention",
    )(pos, q, do, v, base, lr, b)


from jax.sharding import PartitionSpec as P

STRIDE_LENGTH = 0.2


def gradient_kernel(own, nrank, pos_ref, x_ref, lg_ref, rt_ref, out_ref):
    g = dot(lg_ref[...], x_ref[...], TN)
    for c in range(nrank // RANK):
        out_ref[0, c] = jnp.concatenate([g[c * RANK:(c + 1) * RANK], rt_ref[0, c]], axis=1).astype(out_ref.dtype)


def gradients(pos, x, lg, rt, n, dtype):
    T, width = x.shape
    nrank = lg.shape[1]
    shards = 2 * n
    heads, nchain, _, kcols = rt.shape
    cols, kcols = width // shards, heads * kcols // shards
    if heads != shards:
        rt = rt.reshape(heads, nchain, RANK, -1, kcols).transpose(0, 3, 1, 2, 4).reshape(shards, nchain, RANK, kcols)
    grid = pltpu.PrefetchScalarGridSpec(
        num_scalar_prefetch=1, grid=(n,),
        in_specs=[
            pl.BlockSpec((T, cols), lambda i, p: (0, p[i])),
            pl.BlockSpec((T, nrank), lambda i, p: (0, 0)),
            pl.BlockSpec((1, nchain, RANK, kcols), lambda i, p: (p[i], 0, 0, 0)),
        ],
        out_specs=pl.BlockSpec((1, nchain, RANK, cols + kcols), lambda i, p: (i, 0, 0, 0)),
    )
    return pl.pallas_call(
        functools.partial(gradient_kernel, n, nrank), grid_spec=grid,
        out_shape=jax.ShapeDtypeStruct((n, nchain, RANK, cols + kcols), dtype),
        compiler_params=pltpu.CompilerParams(vmem_limit_bytes=24 * 1024 * 1024),
        cost_estimate=pl.CostEstimate(flops=T * width * nrank, bytes_accessed=3_000_000, transcendentals=0),
        name="gradients",
    )(pos, x, lg, rt)


def reorder_kernel(pos_ref, x_ref, out_ref):
    out_ref[...] = x_ref[...]


def reorder(pos, x, cols):
    T, width = x.shape
    grid = pltpu.PrefetchScalarGridSpec(
        num_scalar_prefetch=1, grid=(width // cols,),
        in_specs=[pl.BlockSpec((T, cols), lambda i, p: (0, p[i]))],
        out_specs=pl.BlockSpec((T, cols), lambda i, p: (0, i)),
    )
    return pl.pallas_call(
        reorder_kernel, grid_spec=grid, out_shape=jax.ShapeDtypeStruct(x.shape, x.dtype),
        compiler_params=pltpu.CompilerParams(vmem_limit_bytes=8 * 1024 * 1024),
        cost_estimate=pl.CostEstimate(flops=0, bytes_accessed=64 * T * width, transcendentals=0), name="reorder",
    )(pos, x)


def per_device(layer_activations, rotated_probes, attended_contents, attended_slope, locked_projection,
               first_multipliers, second_multipliers, first_jitter, second_jitter, chain_heats, donor_chain):
    T, width = layer_activations.shape
    scale = 1.0 / math.sqrt(width * RANK)
    nchain, arows, _ = first_multipliers.shape
    nc = lax.axis_size("chain")
    nt = lax.axis_size("tok")
    nz = nt // 2
    p = lax.axis_index("chain")
    t = lax.axis_index("tok")
    z, core = t // 2, t % 2

    def shift(x, k):
        return lax.ppermute(x, "tok", [(i, (i + 2 * k) % nt) for i in range(nt)])

    def swap_cores(x):
        return lax.ppermute(x, "tok", [(i, i ^ 1) for i in range(nt)])

    def exchange(x, k):
        return lax.ppermute(x, "chain", [(i, i ^ k) for i in range(nc)])

    source = lax.dynamic_slice_in_dim(donor_chain, p * nchain, nchain)

    def gather_slots(own):
        return [own] + [exchange(own, k) for k in range(1, nc)]

    def take_slots(parts, source):
        every = jnp.concatenate(parts)
        return jnp.concatenate([
            lax.dynamic_slice_in_dim(every, (source[j] // nchain ^ p) * nchain + source[j] % nchain, 1)
            for j in range(nchain)
        ])

    first = first_multipliers.transpose(0, 2, 1)
    kcols = second_multipliers.shape[2]
    nrank = nchain * RANK

    offsets = [0]
    for k in range(1, nz // 2):
        offsets += [-k, k]
    offsets.append(nz // 2)
    order = []
    for k in offsets:
        order += [(z + k) % nz * 2 + core, (z + k) % nz * 2 + 1 - core]

    def onward(shards, k):
        if k < nz // 2:
            up, down = (shards[-2], shards[-1]) if k > 1 else (shards[0], shards[0])
            return [shift(up, 1), shift(down, -1)]
        return [shift(shards[-2], 1)]

    w = [locked_projection]
    w += onward(w, 1)
    ab_own = jnp.concatenate([first, second_multipliers], axis=2).astype(bf16)
    ab = take_slots(gather_slots(ab_own), source).reshape(nrank, arows + kcols)
    heats, w, ab = lax.optimization_barrier((chain_heats, w, ab))
    up, down = [ab], [ab]
    for k in range(2, nz // 2 + 1):
        w += onward(w, k)
        up.append(shift(up[-1], 1))
    w_there = [swap_cores(x) for x in w[:-1]]
    heat = jnp.sqrt(2.0 * STRIDE_LENGTH * heats)[:, None, None]
    pre_a = (1.0 - STRIDE_LENGTH) * first + heat * first_jitter.transpose(0, 2, 1)
    pre_b = (1.0 - STRIDE_LENGTH) * second_multipliers + heat * second_jitter
    rest_own = jnp.concatenate([pre_a, pre_b], axis=2).astype(bf16)
    rest_own, w_there, order = lax.optimization_barrier((rest_own, w_there, jnp.stack(order).astype(jnp.int32)))
    x_ordered = reorder(order, layer_activations, arows)
    x_ordered, down = lax.optimization_barrier((x_ordered, down))

    def x_piece(s, theirs):
        return x_ordered[:, (2 * s + theirs) * arows:(2 * s + theirs + 1) * arows]

    def add(total, s, here, there, dims):
        for i, x in enumerate((here, there)):
            total = total + dot(x_piece(s, i), x, dims)
        return total

    plain = 0.0
    for s in range(nz - 1):
        plain = add(plain, s, w[s], w_there[s], NN)
    rest_parts = gather_slots(rest_own)
    w[-1], up, w_there, rest_parts = lax.optimization_barrier((w[-1], up, w_there, rest_parts))
    up.append(shift(up[-1], 1))
    for k in range(1, nz // 2):
        down.append(shift(down[-1], -1))
    plain = add(plain, nz - 1, w[-1], swap_cores(w[-1]), NN).astype(bf16)
    base = jnp.stack([plain] + [exchange(plain, k) for k in range(1, nc)])
    a = [ab]
    for k in range(1, nz // 2):
        a += [up[k], down[k]]
    a.append(up[-1])
    low_rank, b_low = 0.0, []
    for s in range(nz):
        if s == 2:
            base, a, low_rank = lax.optimization_barrier((base, a, low_rank))
        there = swap_cores(a[s])
        low_rank = add(low_rank, s, a[s][:, :arows], there[:, :arows], NT)
        b_low += [a[s][:, arows:], there[:, arows:]]
    low_rank = low_rank.astype(bf16)
    shards = jnp.arange(nt, dtype=jnp.int32)
    step_of = jnp.array([[k % nz for k in offsets].index(d) for d in range(nz)], jnp.int32)
    places = step_of[(shards // 2 - z) % nz] * 2 + (shards % 2 != core).astype(jnp.int32)
    pos = jnp.concatenate([p[None], places]).astype(jnp.int32)

    low_grad, right = attention(pos, rotated_probes, attended_slope, attended_contents, base, low_rank, jnp.stack(b_low), scale)

    low_grad, right, rest_parts = lax.optimization_barrier((low_grad, right, rest_parts))
    rest = take_slots(rest_parts, source)
    around = (z + jnp.arange(nz, dtype=jnp.int32)) % nz
    theirs = swap_cores(gradients(around * 2 + 1 - core, layer_activations, low_grad, right, nz, bf16))
    mine = gradients(around * 2 + core, layer_activations, low_grad, right, nz, f32)
    total = mine[0] + theirs[0]
    send = (mine[1:] + theirs[1:]).astype(bf16)
    for k in sorted(range(1, nz), key=lambda k: min(k, nz - k)):
        total = total + shift(send[k - 1], k).astype(f32)
    new = rest.astype(f32) - STRIDE_LENGTH * total
    return new[:, :, :arows].transpose(0, 2, 1), new[:, :, arows:]


def solution(mesh):
    return jax.shard_map(
        per_device,
        mesh=mesh,
        in_specs=(
            P("tok", None), P("tok", None), P("tok", None), P("tok", None), P("tok", "chain"),
            P("chain", "tok", None), P("chain", None, "tok"), P("chain", "tok", None), P("chain", None, "tok"),
            P("chain"), P(),
        ),
        out_specs=(P("chain", "tok", None), P("chain", None, "tok")),
        check_vma=False,
    )
```
